256 devices in a mesh: grp: 8 (over x_lo, y), blk: 32 (over x_hi, z, core).
Axes of the slice: x: 4 (x_hi: 2, x_lo: 2; x = x_hi * 2 + x_lo), y: 4, z: 8, core: 2. Of those that a mesh axis runs over, the one named last changes fastest.
Arguments:
- feat_one: bfloat16 [65536, 256], P(('grp', 'blk')), parts along dimension 0, may hold values from -8 to 8
- feat_two: bfloat16 [65536, 256], P(('grp', 'blk')), parts along dimension 0, may hold values from -8 to 8
- match_one: int32 [256, 256], P(('grp', 'blk')), parts along dimension 0, may hold values from 0 to 255, each once within a row
- match_two: int32 [256, 256], P(('grp', 'blk')), parts along dimension 0, may hold values from 0 to 255, each once within a row
- valid_counts: int32 [256], P(('grp', 'blk')), parts along dimension 0, may hold values from 128 to 256, as said below
Outputs:
- grad_one: float32 [65536, 256], P(('grp', 'blk')), parts along dimension 0
- grad_two: float32 [65536, 256], P(('grp', 'blk')), parts along dimension 0
- row_lse: float32 [65536], P(('grp', 'blk')), parts along dimension 0
- col_lse: float32 [65536], P(('grp', 'blk')), parts along dimension 0
The draws below stay inside these ranges and needn't reach their ends.
There are 8 independent parts, one for each index of `grp`. The reference program is written for one: setup_inputs(seed, part) draws one part's arguments, and reference() takes and returns one part's arrays. A program takes and returns all parts, laid end to end along the dimension named above; each array names one. Nothing has to cross between parts.
Inputs may be any that keep to these rules, and one draw needn't show every extreme that they name: `valid_counts`: at least half of a device's pairs are valid, and some device has all 256 valid.
All inputs are finite; a program needn't handle non-finite values.
Results may differ from the reference program's by a relative error of at most 0.0016.
Values may be sent and summed in bfloat16 or wider, within the bound.
No kernel may reach another device: no remote copies, remote signals or barrier semaphores. Data moves between devices by JAX's collectives and lax.ppermute only.
A program may use at most 64 MiB of HBM per device.

```python
import math
import jax
import jax.numpy as jnp
from jax import lax

D = 256
PAIRS = 256
PTS = 8192
N_BLK = 32


def draw_feat_one(key, part):
    key = jax.random.fold_in(key, 11)
    base = jnp.clip(jax.random.normal(key, (PTS, D), jnp.float32), -6.0, 6.0)
    return base.astype(jnp.bfloat16)


def draw_feat_two(key, part):
    key = jax.random.fold_in(key, 23)
    base = jnp.clip(jax.random.normal(key, (PTS, D), jnp.float32), -6.0, 6.0)
    return base.astype(jnp.bfloat16)


def draw_valid_counts(key, part):
    key = jax.random.fold_in(key, 5)
    first, second = jax.random.split(key)
    counts = jax.random.randint(first, (N_BLK,), PAIRS // 2, PAIRS + 1)
    where_full = jax.random.randint(second, (), 0, N_BLK)
    return jnp.where(jnp.arange(N_BLK) == where_full, PAIRS, counts).astype(jnp.int32)


def setup_inputs(seed: int = 0, part: int = 0) -> dict:
    seeds = jax.random.split(jax.random.key(seed), 6)
    part_keys = jax.random.split(jax.random.fold_in(seeds[5], part), 6)
    feat_one = draw_feat_one(jax.random.fold_in(jax.random.fold_in(seeds[5], part), 71), part)
    feat_two = draw_feat_two(jax.random.fold_in(jax.random.fold_in(seeds[5], part), 71), part)
    match_one = jax.vmap(lambda own: jax.random.permutation(own, PAIRS))(jax.random.split(part_keys[2], N_BLK)).reshape((N_BLK, PAIRS)).astype(jnp.int32)
    match_two = jax.vmap(lambda own: jax.random.permutation(own, PAIRS))(jax.random.split(part_keys[3], N_BLK)).reshape((N_BLK, PAIRS)).astype(jnp.int32)
    valid_counts = draw_valid_counts(jax.random.fold_in(jax.random.fold_in(seeds[5], part), 71), part)
    return {"feat_one": feat_one, "feat_two": feat_two, "match_one": match_one, "match_two": match_two, "valid_counts": valid_counts}


NEG = -1e+30

def lse_of(left, right, right_mask):
    scale = 2.0 / math.sqrt(D)
    rows = left.shape[0]
    size = min(1024, rows)
    blocks = left.reshape(rows // size, size, left.shape[1])

    def one(block):
        s = jnp.dot(block, right.T, preferred_element_type=jnp.float32) * scale
        sv = jnp.where(right_mask[None, :] > 0, s, NEG)
        m = lax.optimization_barrier(jnp.max(sv, axis=1))
        e = jnp.where(right_mask[None, :] > 0, jnp.exp(sv - m[:, None]), 0.0)
        return m + jnp.log(lax.optimization_barrier(jnp.sum(e, axis=1)))
    return lax.map(one, blocks).reshape(rows)

def grad_of(left, left_mask, left_lse, right, right_mask, right_lse):
    scale = 2.0 / math.sqrt(D)
    rows = left.shape[0]
    size = min(1024, rows)
    parts = (left.reshape(rows // size, size, left.shape[1]), left_mask.reshape(rows // size, size), left_lse.reshape(rows // size, size))

    def one(piece):
        block, bmask, blse = piece
        s = jnp.dot(block, right.T, preferred_element_type=jnp.float32) * scale
        keep = (bmask[:, None] > 0) & (right_mask[None, :] > 0)
        w = jnp.where(keep, jnp.exp(s - blse[:, None]) + jnp.exp(s - right_lse[None, :]), 0.0).astype(jnp.bfloat16)
        return jnp.dot(w, right, preferred_element_type=jnp.float32)
    return lax.map(one, parts).reshape(rows, right.shape[1])

def reference(feat_one, feat_two, match_one, match_two, valid_counts):
    base = (jnp.arange(N_BLK, dtype=jnp.int32) * PAIRS)[:, None]
    rows_one = (match_one + base).reshape(PTS).astype(jnp.int32)
    rows_two = (match_two + base).reshape(PTS).astype(jnp.int32)
    query = feat_one[rows_one]
    keys = feat_two[rows_two]
    local = jnp.arange(PAIRS, dtype=jnp.int32)[None, :]
    valid = (local < valid_counts[:, None]).reshape(PTS).astype(jnp.float32)
    row_lse = lse_of(query, keys, valid)
    col_lse = lse_of(keys, query, valid)
    total = jnp.sum(valid_counts).astype(jnp.float32)
    coef = 2.0 / math.sqrt(D) / (2.0 * total)
    dq = coef * (grad_of(query, valid, row_lse, keys, valid, col_lse) - 2.0 * valid[:, None] * keys.astype(jnp.float32))
    dk = coef * (grad_of(keys, valid, col_lse, query, valid, row_lse) - 2.0 * valid[:, None] * query.astype(jnp.float32))
    grad_one = jnp.zeros((PTS, D), jnp.float32).at[rows_one].set(dq)
    grad_two = jnp.zeros((PTS, D), jnp.float32).at[rows_two].set(dk)
    return (grad_one, grad_two, row_lse, col_lse)
```

```python
import math

import jax
import jax.numpy as jnp
from jax import lax
from jax.experimental import pallas as pl
from jax.experimental.pallas import tpu as pltpu
from jax.sharding import PartitionSpec as P

NEG = -1e30
BF = jnp.bfloat16
F32 = jnp.float32
N = 256
PACK = 272
SCALE2 = (2.0 / math.sqrt(256)) * math.log2(math.e)
LN2 = math.log(2.0)
NT = (((1,), (1,)), ((), ()))
NN = (((1,), (0,)), ((), ()))


def dot(a, b, dims):
    return lax.dot_general(a, b, dims, preferred_element_type=F32)


def perm(move):
    pairs = []
    for x in range(2):
        for z in range(8):
            for c in range(2):
                x2, z2, c2 = move(x, z, c)
                pairs.append(((x * 8 + z) * 2 + c, (x2 * 8 + z2 % 8) * 2 + c2))
    return pairs


CORE = perm(lambda x, z, c: (x, z, 1 - c))
XX = perm(lambda x, z, c: (1 - x, z, c))
ZZ = perm(lambda x, z, c: (x, z ^ 1, c))
XZ = perm(lambda x, z, c: (1 - x, z ^ 1, c))
UP2 = perm(lambda x, z, c: (x, z + 2, c))
UP4 = perm(lambda x, z, c: (x, z + 4, c))
UP6 = perm(lambda x, z, c: (x, z + 6, c))


def send(array, pairs):
    return lax.ppermute(array, "blk", pairs)


def eye():
    return lax.broadcasted_iota(jnp.int32, (N, N), 0) == lax.broadcasted_iota(
        jnp.int32, (N, N), 1
    )


def to_column(row, diag):
    return jnp.sum(jnp.where(diag, row, 0.0), axis=1, keepdims=True)


def to_row(column, diag):
    return jnp.sum(jnp.where(diag, column, 0.0), axis=0, keepdims=True)


def merge(a, b):
    top = jnp.maximum(a, b)
    return top + jnp.log2(jnp.exp2(a - top) + jnp.exp2(b - top))


def onehot(match_ref):
    return lax.broadcasted_iota(jnp.int32, (N, N), 0) == match_ref[...]


def pack_kernel(count_ref, m1_ref, m2_ref, f1_ref, f2_ref, q_ref, k_ref):
    valid = (lax.broadcasted_iota(jnp.int32, (16, N), 1) < count_ref[0]).astype(F32).astype(BF)
    for m_ref, f_ref, o_ref in ((m1_ref, f1_ref, q_ref), (m2_ref, f2_ref, k_ref)):
        pick = onehot(m_ref).astype(F32).astype(BF)
        o_ref[:N, :] = f_ref[...]
        o_ref[N:, :] = dot(valid, pick, NT).astype(BF)


def pair_kernel(count_ref, m1_ref, m2_ref, f1_ref, f2_ref, pk_ref, pq_ref):
    valid = lax.broadcasted_iota(jnp.int32, (N, N), 1) < count_ref[0]
    one = onehot(m1_ref)
    two = onehot(m2_ref)
    one_valid = (one & valid).astype(F32).astype(BF)
    two_valid = (two & valid).astype(F32).astype(BF)
    to_one = dot(one_valid, two.astype(F32).astype(BF), NT).astype(BF)
    to_two = dot(two_valid, one.astype(F32).astype(BF), NT).astype(BF)
    pk_ref[...] = dot(to_one, f2_ref[...], NN)
    pq_ref[...] = dot(to_two, f1_ref[...], NN)


def load_blocks(q_refs, k_refs, q_all, k_all, q_mask, k_bias):
    for i, ref in enumerate(q_refs):
        q_all[i * N : (i + 1) * N, :] = ref[:N, :]
        q_mask[i : i + 1, :] = ref[N:, :].astype(F32)[:1, :]
    for j, ref in enumerate(k_refs):
        k_all[j * N : (j + 1) * N, :] = ref[:N, :]
        k_bias[:, j * N : (j + 1) * N] = (1.0 - ref[N:, :].astype(F32)[:1, :]) * NEG


def stats_kernel(*refs):
    q_refs, k_refs = refs[:8], refs[8:12]
    rl_ref, cl_ref, q_all, k_all, q_mask, k_bias = refs[12:]
    load_blocks(q_refs, k_refs, q_all, k_all, q_mask, k_bias)
    diag = eye()

    def step(i, carry):
        col_max, col_sum = carry
        q = q_all[pl.ds(pl.multiple_of(i * N, N), N), :]
        t = dot(q, k_all[...], NT) * SCALE2
        row_bias = (1.0 - to_column(q_mask[pl.ds(i, 1), :], diag)) * NEG
        a = t + k_bias[...]
        row_max = jnp.max(a, axis=1, keepdims=True)
        row_sum = jnp.sum(jnp.exp2(a - row_max), axis=1, keepdims=True)
        rl_ref[pl.ds(i, 1), :] = to_row(row_max + jnp.log2(row_sum), diag)
        b = t + row_bias
        top = jnp.max(b, axis=0, keepdims=True)
        new_max = jnp.maximum(col_max, top)
        new_sum = col_sum * jnp.exp2(col_max - new_max) + jnp.sum(
            jnp.exp2(b - new_max), axis=0, keepdims=True
        )
        return new_max, new_sum

    width = 4 * N
    col_max, col_sum = lax.fori_loop(
        0, 8, step, (jnp.full((1, width), NEG, F32), jnp.zeros((1, width), F32))
    )
    col_lse = col_max + jnp.log2(col_sum)
    cl_ref[...] = jnp.zeros((8, N), F32) + jnp.sum(q_mask[...])
    for j in range(4):
        cl_ref[j : j + 1, :] = col_lse[:, j * N : (j + 1) * N]


def core_kernel(a_ref, b_ref, o_ref):
    b = b_ref[...]
    o_ref[...] = merge(a_ref[...], jnp.concatenate([b[4:], b[:4]], axis=0))


def grad_kernel(*refs):
    q_refs, k_refs, r_refs, c_refs = refs[:8], refs[8:12], refs[12:16], refs[16:20]
    dq_own, dq_other, dk_own, dk1, dk2, dk3, lse_ref = refs[20:27]
    q_all, k_all, q_mask, k_bias, row_lse, acc = refs[27:]
    load_blocks(q_refs, k_refs, q_all, k_all, q_mask, k_bias)
    diag = eye()
    rows = r_refs[0][...]
    for step, ref in enumerate(r_refs[1:], start=1):
        other = ref[...]
        order = [i ^ step for i in range(8)]
        other = jnp.concatenate([other[i : i + 1] for i in order], axis=0)
        rows = merge(rows, other)
    row_lse[...] = rows
    cols = c_refs[0][...]
    total = cols[7:8, :]
    parts = [cols[j : j + 1] for j in range(4)]
    for step, ref in enumerate(c_refs[1:], start=1):
        other = ref[...]
        total = total + other[7:8, :]
        parts = [merge(parts[j], other[(j - step) % 4 : (j - step) % 4 + 1]) for j in range(4)]
    lse_ref[...] = jnp.concatenate(
        [rows[:1], parts[0], total, jnp.zeros((5, N), F32)], axis=0
    )
    col_lse = jnp.concatenate(parts, axis=1)
    acc[...] = jnp.zeros_like(acc)

    def step(i, carry):
        q = q_all[pl.ds(pl.multiple_of(i * N, N), N), :]
        t = dot(q, k_all[...], NT) * SCALE2
        row_bias = (1.0 - to_column(q_mask[pl.ds(i, 1), :], diag)) * NEG
        row = to_column(row_lse[pl.ds(i, 1), :], diag)
        t = t + row_bias + k_bias[...]
        w = (jnp.exp2(t - row) + jnp.exp2(t - col_lse)).astype(BF)
        dq = dot(w, k_all[...], NN)

        @pl.when(i < 4)
        def _():
            dq_own[pl.ds(pl.multiple_of(i * N, N), N), :] = dq

        @pl.when(i >= 4)
        def _():
            dq_other[pl.ds(pl.multiple_of((i - 4) * N, N), N), :] = dq.astype(BF)

        acc[...] += dot(q.astype(F32).T.astype(BF), w, NN)
        return carry

    lax.fori_loop(0, 8, step, 0)
    dk_own[...] = acc[:, :N]
    for j, ref in enumerate((dk1, dk2, dk3), start=1):
        ref[...] = acc[:, j * N : (j + 1) * N].astype(BF)


def core_sum_kernel(own_ref, other_ref, a_ref, b1_ref, b2_ref, b3_ref):
    for i, ref in enumerate((a_ref, b1_ref, b2_ref, b3_ref)):
        block = slice(i * N, (i + 1) * N)
        ref[...] = (own_ref[block, :] + other_ref[block, :].astype(F32)).astype(ref.dtype)


def final_kernel(m1_ref, m2_ref, lse_ref, pk_ref, pq_ref, a0, a1, a2, a3, b0, b1, b2, b3, *outs):
    g1, g2, rl, cl = outs
    total = lse_ref[2:3, :1]
    coef = (2.0 / math.sqrt(N)) / (2.0 * total)
    acc = a0[...] + a1[...].astype(F32) + a2[...].astype(F32) + a3[...].astype(F32)
    g1[...] = coef * (acc - 2.0 * pk_ref[...])
    acc = b0[...] + b1[...].astype(F32) + b2[...].astype(F32) + b3[...].astype(F32)
    g2[...] = coef * (acc.T - 2.0 * pq_ref[...])
    diag = eye()
    for at, m_ref, out in ((0, m1_ref, rl), (1, m2_ref, cl)):
        column = to_column(lse_ref[at : at + 1, :], diag)
        out[...] = jnp.sum(jnp.where(onehot(m_ref), column, 0.0), axis=0, keepdims=True) * LN2


def vmem(n):
    return [pl.BlockSpec(memory_space=pltpu.VMEM)] * n


def call(kernel, ins, outs, scratch=(), smem=0, flops=0, trans=0, limit=32):
    return pl.pallas_call(
        kernel,
        out_shape=[jax.ShapeDtypeStruct(s, d) for s, d in outs],
        in_specs=[pl.BlockSpec(memory_space=pltpu.SMEM)] * smem + vmem(len(ins) - smem),
        out_specs=vmem(len(outs)),
        scratch_shapes=list(scratch),
        compiler_params=pltpu.CompilerParams(vmem_limit_bytes=limit * 2**20),
        cost_estimate=pl.CostEstimate(flops=flops, bytes_accessed=2**20, transcendentals=trans),
    )(*ins)


def local(feat_one, feat_two, match_one, match_two, valid_counts):
    ins = (valid_counts, match_one, match_two, feat_one, feat_two)
    qm, km = call(pack_kernel, ins, [((PACK, N), BF)] * 2, smem=1)
    k_all = [km, send(km, UP6), send(km, UP4), send(km, UP2)]
    q_all = [qm, send(qm, XX), send(qm, ZZ), send(qm, XZ)]
    q_all += [send(a, CORE) for a in q_all]
    pk, pq = call(pair_kernel, ins, [((N, N), F32)] * 2, smem=1)
    blocks = [
        pltpu.VMEM((8 * N, N), BF),
        pltpu.VMEM((4 * N, N), BF),
        pltpu.VMEM((8, N), F32),
        pltpu.VMEM((1, 4 * N), F32),
    ]
    size = 2 * 2048 * 1024 * 256
    rl, cl = call(
        stats_kernel, q_all + k_all, [((8, N), F32)] * 2, blocks, flops=size, trans=2**22
    )
    rl_other = send(rl, CORE)
    cl_all = [cl, send(cl, UP2), send(cl, UP4), send(cl, UP6)]
    cl_all = [cl_all[0], cl_all[3], cl_all[2], cl_all[1]]
    (rl,) = call(core_kernel, (rl, rl_other), [((8, N), F32)])
    rl_all = [rl, send(rl, XX), send(rl, ZZ), send(rl, XZ)]
    out = [((4 * N, N), F32), ((4 * N, N), BF), ((N, N), F32)] + [((N, N), BF)] * 3
    dq_own, dq_other, dk0, dk1, dk2, dk3, lse = call(
        grad_kernel,
        q_all + k_all + rl_all + cl_all,
        out + [((8, N), F32)],
        blocks + [pltpu.VMEM((8, N), F32), pltpu.VMEM((N, 4 * N), F32)],
        flops=3 * size,
        trans=2**22,
    )
    dk = [dk0, send(dk1, UP2), send(dk2, UP4), send(dk3, UP6)]
    dq_other = send(dq_other, CORE)
    dq = call(
        core_sum_kernel, (dq_own, dq_other), [((N, N), F32)] + [((N, N), BF)] * 3
    )
    dq = [dq[0], send(dq[1], XX), send(dq[2], ZZ), send(dq[3], XZ)]
    grad_one, grad_two, row_lse, col_lse = call(
        final_kernel,
        [match_one, match_two, lse, pk, pq] + dq + dk,
        [((N, N), F32)] * 2 + [((1, N), F32)] * 2,
    )
    return grad_one, grad_two, row_lse.reshape(N), col_lse.reshape(N)


def solution(mesh):
    both = ("grp", "blk")
    return jax.shard_map(
        local,
        mesh=mesh,
        in_specs=(P(both, None),) * 4 + (P(both),),
        out_specs=(P(both, None), P(both, None), P(both), P(both)),
        check_vma=False,
    )
```

```python
import math

import jax
import jax.numpy as jnp
from jax import lax
from jax.experimental import pallas as pl
from jax.experimental.pallas import tpu as pltpu
from jax.sharding import PartitionSpec as P

NEG = -1e30
BF = jnp.bfloat16
F32 = jnp.float32
N = 256
PACK = 272
SCALE2 = (2.0 / math.sqrt(256)) * math.log2(math.e)
LN2 = math.log(2.0)
NT = (((1,), (1,)), ((), ()))
NN = (((1,), (0,)), ((), ()))
ARRIVAL = [(0, 0), (0, 1)]
for hop in (1, 2, 3):
    ARRIVAL += [(-hop, 0), (hop, 0), (-hop, 1), (hop, 1)]
ARRIVAL += [(-4, 0), (4, 1)]


def dot(a, b, dims):
    return lax.dot_general(a, b, dims, preferred_element_type=F32)


def perm(move):
    pairs = []
    for x in range(2):
        for z in range(8):
            for c in range(2):
                x2, z2, c2 = move(x, z, c)
                pairs.append(((x * 8 + z) * 2 + c, (x2 * 8 + z2 % 8) * 2 + c2))
    return pairs


CORE = perm(lambda x, z, c: (x, z, 1 - c))
XX = perm(lambda x, z, c: (1 - x, z, c))
UP = perm(lambda x, z, c: (x, z + 1, c))
DOWN = perm(lambda x, z, c: (x, z - 1, c))


def send(array, pairs):
    return lax.ppermute(array, "blk", pairs)


def place():
    me = lax.axis_index("blk")
    return me // 16, (me // 2) % 8, me % 2


def eye():
    return lax.broadcasted_iota(jnp.int32, (N, N), 0) == lax.broadcasted_iota(
        jnp.int32, (N, N), 1
    )


def to_column(row, diag):
    return jnp.sum(jnp.where(diag, row, 0.0), axis=1, keepdims=True)


def merge(a, b):
    top = jnp.maximum(a, b)
    return top + jnp.log2(jnp.exp2(a - top) + jnp.exp2(b - top))


def onehot(match_ref):
    return lax.broadcasted_iota(jnp.int32, (N, N), 0) == match_ref[...]


def pack_kernel(count_ref, m1_ref, m2_ref, f1_ref, f2_ref, x_ref, y_ref):
    first = place()[2] == 0
    valid = (lax.broadcasted_iota(jnp.int32, (16, N), 1) < count_ref[0]).astype(F32).astype(BF)

    def write(m_ref, f_ref, o_ref):
        pick = onehot(m_ref).astype(F32).astype(BF)
        o_ref[:N, :] = f_ref[...]
        o_ref[N:, :] = dot(valid, pick, NT).astype(BF)

    @pl.when(first)
    def _():
        write(m1_ref, f1_ref, x_ref)
        write(m2_ref, f2_ref, y_ref)

    @pl.when(jnp.logical_not(first))
    def _():
        write(m2_ref, f2_ref, x_ref)
        write(m1_ref, f1_ref, y_ref)


def pair_kernel(count_ref, m1_ref, m2_ref, f1_ref, f2_ref, pk_ref, pq_ref):
    valid = lax.broadcasted_iota(jnp.int32, (N, N), 1) < count_ref[0]
    one = onehot(m1_ref)
    two = onehot(m2_ref)
    one_valid = (one & valid).astype(F32).astype(BF)
    two_valid = (two & valid).astype(F32).astype(BF)
    to_one = dot(one_valid, two.astype(F32).astype(BF), NT).astype(BF)
    to_two = dot(two_valid, one.astype(F32).astype(BF), NT).astype(BF)
    pk_ref[...] = dot(to_one, f2_ref[...], NN)
    pq_ref[...] = dot(to_two, f1_ref[...], NN)


def stats_kernel(first, last, *refs):
    x_refs, refs = refs[:4], refs[4:]
    if not first:
        carry_ref, refs = refs[0], refs[1:]
    y_refs, o_ref, x_all = refs[:-2], refs[-2], refs[-1]
    for i, ref in enumerate(x_refs):
        x_all[i * N : (i + 1) * N, :] = ref[:N, :]
    diag = eye()
    width = 4 * N
    if first:
        top = jnp.full((1, width), NEG, F32)
        total = jnp.zeros((1, width), F32)
        count = jnp.zeros((1, 1), F32)
    else:
        top = carry_ref[0:1, :]
        total = carry_ref[1:2, :]
        count = carry_ref[2:3, :1]
    for ref in y_refs:
        mask = ref[N:, :].astype(F32)[:1, :]
        count = count + jnp.sum(mask, axis=1, keepdims=True)
        bias = (1.0 - to_column(mask, diag)) * NEG
        t = dot(ref[:N, :], x_all[...], NT) * SCALE2 + bias
        new = jnp.maximum(top, jnp.max(t, axis=0, keepdims=True))
        total = total * jnp.exp2(top - new) + jnp.sum(jnp.exp2(t - new), axis=0, keepdims=True)
        top = new
    if last:
        o_ref[:, :width] = top + jnp.log2(total)
        o_ref[:, width:] = jnp.broadcast_to(count, (1, 128))
    else:
        o_ref[0:1, :] = top
        o_ref[1:2, :] = total
        o_ref[2:3, :] = jnp.broadcast_to(count, (1, width))


def grad_kernel(pair, *refs):
    recv, x_refs, y_refs, refs = refs[0], refs[1:3], refs[3:19], refs[19:]
    d_ref, refs = refs[0], refs[1:]
    if pair == 0:
        lse_ref, refs = refs[0], refs[1:]
    y_all, bias, col = refs
    x, z, c = place()

    def source(x1, z1, c1):
        return recv[(x1 * 8 + z1) * 2 + c1]

    for j, (ref, (offset, chain)) in enumerate(zip(y_refs, ARRIVAL)):
        block = slice(j * N, (j + 1) * N)
        y_all[block, :] = ref[:N, :]
        bias[:, block] = (1.0 - ref[N:, :].astype(F32)[:1, :]) * NEG
        z1 = lax.rem(z + offset + 8, 8)
        near = 1 - chain
        col[:, block] = merge(
            source(x, z1, 1 - c)[:, near * N : (near + 1) * N],
            source(1 - x, z1, 1 - c)[:, (near + 2) * N : (near + 3) * N],
        )
    mine = source(x, z, c)
    theirs = source(1 - x, z, c)
    diag = eye()
    for i in range(2):
        at = 2 * pair + i
        other = (at + 2) % 4
        row = merge(mine[:, at * N : (at + 1) * N], theirs[:, other * N : (other + 1) * N])
        if pair == 0 and i == 0:
            total = mine[:, 4 * N :][:, :1] + theirs[:, 4 * N :][:, :1]
            lse_ref[...] = jnp.concatenate(
                [row, col[:, :N], jnp.broadcast_to(total, (1, N)), jnp.zeros((5, N), F32)], axis=0
            )
        row = to_column(row, diag)
        xb = x_refs[i][:N, :]

        def step(j, acc):
            block = pl.ds(pl.multiple_of(j * 1024, 1024), 1024)
            y = y_all[block, :]
            t = dot(xb, y, NT) * SCALE2 + bias[:, block]
            w = (jnp.exp2(t - row) + jnp.exp2(t - col[:, block])).astype(BF)
            return acc + dot(w, y, NN)

        acc = lax.fori_loop(0, 4, step, jnp.zeros((N, N), F32))
        d_ref[i * N : (i + 1) * N, :] = acc.astype(d_ref.dtype)


def sum_kernel(own_ref, other_ref, b_ref):
    b_ref[...] = own_ref[N:, :] + other_ref[N:, :].astype(F32)


def final_kernel(count_ref, m1_ref, m2_ref, lse_ref, pk_ref, pq_ref, own_ref, other_ref, b_ref, *outs):
    g1, g2, rl, cl = outs
    coef = (2.0 / math.sqrt(N)) / (2.0 * lse_ref[2:3, :1])
    near = own_ref[:N, :] + other_ref[:N, :].astype(F32)
    far = b_ref[...]
    valid = lax.broadcasted_iota(jnp.int32, (N, N), 1) < count_ref[0]
    diag = eye()

    def write(m_ref, acc, pair_ref, at, g_ref, l_ref):
        pick = onehot(m_ref)
        live = jnp.sum(jnp.where(pick & valid, 1.0, 0.0), axis=1, keepdims=True) > 0.0
        g_ref[...] = coef * (jnp.where(live, acc, 0.0) - 2.0 * pair_ref[...])
        column = to_column(lse_ref[at : at + 1, :], diag)
        l_ref[...] = jnp.sum(jnp.where(pick, column, 0.0), axis=0, keepdims=True) * LN2

    first = place()[2] == 0

    @pl.when(first)
    def _():
        write(m1_ref, near, pk_ref, 0, g1, rl)
        write(m2_ref, far, pq_ref, 1, g2, cl)

    @pl.when(jnp.logical_not(first))
    def _():
        write(m1_ref, far, pk_ref, 1, g1, rl)
        write(m2_ref, near, pq_ref, 0, g2, cl)


def vmem(n):
    return [pl.BlockSpec(memory_space=pltpu.VMEM)] * n


def call(kernel, ins, outs, scratch=(), smem=0, flops=0, trans=0, limit=32):
    return pl.pallas_call(
        kernel,
        out_shape=[jax.ShapeDtypeStruct(s, d) for s, d in outs],
        in_specs=[pl.BlockSpec(memory_space=pltpu.SMEM)] * smem + vmem(len(ins) - smem),
        out_specs=vmem(len(outs)),
        scratch_shapes=list(scratch),
        compiler_params=pltpu.CompilerParams(vmem_limit_bytes=limit * 2**20),
        cost_estimate=pl.CostEstimate(flops=flops, bytes_accessed=2**20, transcendentals=trans),
    )(*ins)


def stats(first, last, xs, ys, carry):
    def kernel(*refs):
        stats_kernel(first, last, *refs)

    shape = (1, 1152) if last else (8, 4 * N)
    ins = list(xs) + ([] if first else [carry]) + list(ys)
    work = len(ys) * 4 * N**3
    (out,) = call(
        kernel, ins, [(shape, F32)], [pltpu.VMEM((4 * N, N), BF)], flops=2 * work, trans=work // N
    )
    return out


def grads(pair, recv, xs, ys):
    def kernel(*refs):
        grad_kernel(pair, *refs)

    outs = [((2 * N, N), F32), ((8, N), F32)] if pair == 0 else [((2 * N, N), BF)]
    scratch = [
        pltpu.VMEM((16 * N, N), BF),
        pltpu.VMEM((1, 16 * N), F32),
        pltpu.VMEM((1, 16 * N), F32),
    ]
    work = 32 * N**3
    return call(
        kernel, [recv] + list(xs) + list(ys), outs, scratch, flops=4 * work, trans=2 * work // N
    )


def local(feat_one, feat_two, match_one, match_two, valid_counts):
    ins = (valid_counts, match_one, match_two, feat_one, feat_two)
    xa, ya = call(pack_kernel, ins, [((PACK, N), BF)] * 2, smem=1)
    yb = send(xa, CORE)
    xb = send(ya, CORE)
    xs = [xa, xb, send(xa, XX), send(xb, XX)]
    ups, downs = [[ya, yb]], [[ya, yb]]
    for hop in range(3):
        ups.append([send(a, UP) for a in ups[-1]])
        downs.append([send(a, DOWN) for a in downs[-1]])
    groups = [[ya, yb]]
    for hop in (1, 2, 3):
        groups.append([ups[hop][0], downs[hop][0], ups[hop][1], downs[hop][1]])
    groups.append([send(ups[3][0], UP), send(downs[3][1], DOWN)])
    carry = None
    for i, ys in enumerate(groups):
        carry = stats(i == 0, i == 4, xs, ys, carry)
    recv = lax.all_to_all(jnp.broadcast_to(carry[None], (32, 1, 1152)), "blk", 0, 0)
    ys = [y for group in groups for y in group]
    (away,) = grads(1, recv, xs[2:], ys)
    away = send(away, XX)
    own, lse = grads(0, recv, xs[:2], ys)
    (b,) = call(sum_kernel, (own, away), [((N, N), F32)])
    b = send(b, CORE)
    pk, pq = call(pair_kernel, ins, [((N, N), F32)] * 2, smem=1)
    grad_one, grad_two, row_lse, col_lse = call(
        final_kernel,
        [valid_counts, match_one, match_two, lse, pk, pq, own, away, b],
        [((N, N), F32)] * 2 + [((1, N), F32)] * 2,
        smem=1,
    )
    return grad_one, grad_two, row_lse.reshape(N), col_lse.reshape(N)


def solution(mesh):
    both = ("grp", "blk")
    return jax.shard_map(
        local,
        mesh=mesh,
        in_specs=(P(both, None),) * 4 + (P(both),),
        out_specs=(P(both, None), P(both, None), P(both), P(both)),
        check_vma=False,
    )
```

```python
import math

import jax
import jax.numpy as jnp
from jax import lax
from jax.experimental import pallas as pl
from jax.experimental.pallas import tpu as pltpu
from jax.sharding import PartitionSpec as P

NEG = -1e30
BF = jnp.bfloat16
F32 = jnp.float32
N = 256
SCALE2 = (2.0 / math.sqrt(256)) * math.log2(math.e)
LN2 = math.log(2.0)
NT = (((1,), (1,)), ((), ()))
NN = (((1,), (0,)), ((), ()))
MARK = 1024.0
ARRIVAL = [(0, 0), (0, 1)]
for hop in (1, 2, 3):
    ARRIVAL += [(-hop, 0), (hop, 0), (-hop, 1), (hop, 1)]
ARRIVAL += [(-4, 0), (4, 1)]
CALLS = (10, 4, 2)


def dot(a, b, dims):
    return lax.dot_general(a, b, dims, preferred_element_type=F32)


def perm(move):
    pairs = []
    for x in range(2):
        for z in range(8):
            for c in range(2):
                x2, z2, c2 = move(x, z, c)
                pairs.append(((x * 8 + z) * 2 + c, (x2 * 8 + z2 % 8) * 2 + c2))
    return pairs


ROLE = perm(lambda x, z, c: (x, z, 1 - c))
HALF = perm(lambda x, z, c: (1 - x, z, c))
UP = perm(lambda x, z, c: (x, z + 1, c))
DOWN = perm(lambda x, z, c: (x, z - 1, c))


def send(array, pairs):
    return lax.ppermute(array, "blk", pairs)


def place():
    me = lax.axis_index("blk")
    return me % 2, me // 16, (me // 2) % 8


def eye():
    return lax.broadcasted_iota(jnp.int32, (N, N), 0) == lax.broadcasted_iota(
        jnp.int32, (N, N), 1
    )


def to_column(row, diag):
    return jnp.sum(jnp.where(diag, row, 0.0), axis=1, keepdims=True)


def merge(a, b):
    top = jnp.maximum(a, b)
    return top + jnp.log2(jnp.exp2(a - top) + jnp.exp2(b - top))


def onehot(match):
    return lax.broadcasted_iota(jnp.int32, (N, N), 0) == match


def to_row(column, diag):
    return jnp.sum(jnp.where(diag, column, 0.0), axis=0, keepdims=True)


def live_column(pick, count):
    valid = lax.broadcasted_iota(jnp.int32, (N, N), 1) < count
    return jnp.sum(jnp.where(pick & valid, 1.0, 0.0), axis=1, keepdims=True) > 0.0


def x_of(ref):
    return ref[:N, :]


def y_of(ref):
    return ref[ref.shape[0] - N :, :]


def fetch(hbm, held, sems):
    copies = [
        pltpu.make_async_copy(src, dst, sems.at[i]) for i, (src, dst) in enumerate(zip(hbm, held))
    ]
    for copy in copies:
        copy.start()
    for copy in copies:
        copy.wait()


def pack_kernel(count_ref, *refs):
    hbm, outs, held, sems = refs[:4], refs[4:10], refs[10:14], refs[14]
    own_ref, x_ref, y_ref, give_x, give_y, match_ref = outs
    fetch(hbm, held, sems)
    m1, m2, f1, f2 = held

    def masked(m_ref, f_ref):
        live = live_column(onehot(m_ref[...]), count_ref[0])
        return jnp.where(live, f_ref[...].astype(F32), MARK).astype(BF)

    def write(mx, fx, my, fy):
        y = masked(my, fy)
        y_ref[...] = y
        own_ref[N:, :] = y
        own_ref[:N, :] = fx[...]
        x_ref[...] = fx[...]
        give_x[...] = masked(mx, fx)
        give_y[...] = fy[...]
        match_ref[...] = jnp.concatenate([mx[...], my[...], jnp.zeros((6, N), jnp.int32)], axis=0)

    role, _, _ = place()

    @pl.when(role == 0)
    def _():
        write(m1, f1, m2, f2)

    @pl.when(role != 0)
    def _():
        write(m2, f2, m1, f1)


def stats_kernel(first, last, *refs):
    x_refs, refs = refs[:4], refs[4:]
    if not first:
        carry_ref, refs = refs[0], refs[1:]
    outs = 3 if last else 2
    y_refs, (o_ref, bias_ref, *message_ref) = refs[:-outs], refs[-outs:]
    diag = eye()
    count = jnp.zeros((1, 1), F32) if first else carry_ref[2:3, :1]
    chunks = []
    for j in range(0, len(y_refs), 2):
        y = jnp.concatenate([y_of(y_refs[j]), y_of(y_refs[j + 1])], axis=0)
        bias = jnp.where(y[:, :1].astype(F32) > 100.0, NEG, 0.0)
        count = count + jnp.sum(jnp.where(bias < 0.0, 0.0, 1.0), axis=0, keepdims=True)
        for k in range(2):
            block = slice((j + k) * N, (j + k + 1) * N)
            bias_ref[:, block] = to_row(bias[k * N : (k + 1) * N], diag)
        chunks.append((y, bias))
    _, half, _ = place()
    for i in range(4):
        block = slice(i * N, (i + 1) * N)
        if first:
            top = jnp.full((1, N), NEG, F32)
            total = jnp.zeros((1, N), F32)
        else:
            top = carry_ref[0:1, block]
            total = carry_ref[1:2, block]
        for y, bias in chunks:
            t = dot(y, x_of(x_refs[i]), NT) * SCALE2 + bias
            new = jnp.maximum(top, jnp.max(t, axis=0, keepdims=True))
            total = total * jnp.exp2(top - new) + jnp.sum(
                jnp.exp2(t - new), axis=0, keepdims=True
            )
            top = new
        if last:
            lse = top + jnp.log2(total)
            o_ref[:, block] = lse
            rows = pl.ds((half if i < 2 else 1 - half) * 16, 16)
            message_ref[0][rows, :, (i % 2) * N : (i % 2 + 1) * N] = jnp.broadcast_to(
                lse[None], (16, 1, N)
            )
        else:
            o_ref[0:1, block] = top
            o_ref[1:2, block] = total
    if last:
        o_ref[:, 4 * N :] = jnp.broadcast_to(count, (1, 128))
    else:
        o_ref[2:3, :] = jnp.broadcast_to(count, (1, 4 * N))


def lse_row(at, own_ref, other_ref):
    other = (at + 2) % 4
    return merge(
        own_ref[:, at * N : (at + 1) * N], other_ref[:, other * N : (other + 1) * N]
    )


def lse_column(recv, z, chain):
    role, half, _ = place()
    near = slice((1 - chain) * N, (2 - chain) * N)
    source = 2 * z + 1 - role
    return merge(recv[half * 16 + source][:, near], recv[(1 - half) * 16 + source][:, near])


def bias_of(bias_refs, j):
    for ref, count in zip(bias_refs, CALLS):
        if j < count:
            return ref[:, j * N : (j + 1) * N]
        j -= count


def ordered(match, lse, diag):
    column = to_column(lse, diag)
    return jnp.sum(jnp.where(onehot(match), column, 0.0), axis=0, keepdims=True) * LN2


def grad_kernel(pair, recv, own_lse, other_lse, match_ref, x0_ref, x1_ref, *refs):
    y_refs, bias_refs, d_refs = refs[:16], refs[16:19], refs[19:]
    role, _, z = place()
    diag = eye()
    cols = [
        lse_column(recv, lax.rem(z + offset + 8, 8), chain) for offset, chain in ARRIVAL
    ]
    for i in range(2):
        row = to_column(lse_row(2 * pair + i, own_lse, other_lse), diag)
        xb = x_of((x0_ref, x1_ref)[i])
        acc = jnp.zeros((N, N), F32)
        for j, col in enumerate(cols):
            y = y_of(y_refs[j])
            t = dot(xb, y, NT) * SCALE2 + bias_of(bias_refs, j)
            w = (jnp.exp2(t - row) + jnp.exp2(t - col)).astype(BF)
            acc = acc + dot(w, y, NN)
        if pair == 0:
            d_refs[i][...] = acc
        else:
            d_refs[0][i * N : (i + 1) * N, :] = acc.astype(BF)
    if pair == 0:
        lse_x = ordered(match_ref[0:1, :], lse_row(0, own_lse, other_lse), diag)
        lse_y = ordered(match_ref[1:2, :], cols[0], diag)
        d_refs[2][...] = jnp.where(role == 0, lse_x, lse_y)
        d_refs[3][...] = jnp.where(role == 0, lse_y, lse_x)


def sum_kernel(d0_ref, d1_ref, away_ref, x_ref, y_ref):
    x_ref[...] = d0_ref[...] + away_ref[:N, :].astype(F32)
    y_ref[...] = d1_ref[...] + away_ref[N:, :].astype(F32)


def scale_of(own_lse, other_lse):
    total = own_lse[:, 4 * N :][:, :1] + other_lse[:, 4 * N :][:, :1]
    return (2.0 / math.sqrt(N)) / (2.0 * total)


def pair_kernel(count_ref, match_ref, fx_ref, fy_ref, px_ref, py_ref):
    valid = lax.broadcasted_iota(jnp.int32, (N, N), 1) < count_ref[0]
    pick_x = onehot(match_ref[0:1, :]).astype(F32)
    pick_y = onehot(match_ref[1:2, :]).astype(F32)
    to_x = dot(jnp.where(valid, pick_x, 0.0).astype(BF), pick_y.astype(BF), NT).astype(BF)
    to_y = dot(jnp.where(valid, pick_y, 0.0).astype(BF), pick_x.astype(BF), NT).astype(BF)
    px_ref[...] = dot(to_x, fy_ref[...], NN)
    py_ref[...] = dot(to_y, x_of(fx_ref), NN)


def final_kernel(count_ref, match_ref, own_lse, other_lse, px_ref, py_ref, dx_ref, dy_ref, g1, g2):
    role, _, _ = place()
    coef = scale_of(own_lse, other_lse)

    def grad_of(match, total, pair):
        live = live_column(onehot(match), count_ref[0])
        return coef * (jnp.where(live, total, 0.0) - 2.0 * pair)

    def write(gx, gy):
        gx[...] = grad_of(match_ref[0:1, :], dx_ref[...], px_ref[...])
        gy[...] = grad_of(match_ref[1:2, :], dy_ref[...], py_ref[...])

    @pl.when(role == 0)
    def _():
        write(g1, g2)

    @pl.when(role != 0)
    def _():
        write(g2, g1)


def vmem(n):
    return [pl.BlockSpec(memory_space=pltpu.VMEM)] * n


def call(kernel, ins, outs, scratch=(), smem=0, hbm=0, limit=32):
    return pl.pallas_call(
        kernel,
        out_shape=[jax.ShapeDtypeStruct(s, d) for s, d in outs],
        in_specs=[pl.BlockSpec(memory_space=pltpu.SMEM)] * smem
        + [pl.BlockSpec(memory_space=pltpu.HBM)] * hbm
        + vmem(len(ins) - smem - hbm),
        out_specs=vmem(len(outs)),
        scratch_shapes=list(scratch),
        compiler_params=pltpu.CompilerParams(vmem_limit_bytes=limit * 2**20),
        cost_estimate=pl.CostEstimate(flops=0, bytes_accessed=2**16, transcendentals=0),
    )(*ins)


def stats(first, last, xs, ys, carry):
    def kernel(*refs):
        stats_kernel(first, last, *refs)

    outs = [((1, 1152) if last else (8, 4 * N), F32), ((1, len(ys) * N), F32)]
    if last:
        outs.append(((32, 1, 2 * N), F32))
    return call(kernel, list(xs) + ([] if first else [carry]) + list(ys), outs)


def grads(pair, recv, lses, match, xs, ys, biases):
    def kernel(*refs):
        grad_kernel(pair, *refs)

    outs = [((2 * N, N), BF)] if pair else [((N, N), F32)] * 2 + [((1, N), F32)] * 2
    return call(kernel, [recv, *lses, match, *xs] + ys + biases, outs)


def local(feat_one, feat_two, match_one, match_two, valid_counts):
    held = [pltpu.VMEM((1, N), jnp.int32)] * 2 + [pltpu.VMEM((N, N), BF)] * 2
    held += [pltpu.SemaphoreType.DMA((4,))]
    own, xa, ya, give_x, give_y, match = call(
        pack_kernel,
        (valid_counts, match_one, match_two, feat_one, feat_two),
        [((2 * N, N), BF)] + [((N, N), BF)] * 4 + [((8, N), jnp.int32)],
        held,
        smem=1,
        hbm=4,
        limit=60,
    )
    yb, xb = send(give_x, ROLE), send(give_y, ROLE)
    ups, downs = [[ya, yb]], [[ya, yb]]
    for hop in range(3):
        ups.append([send(a, UP) for a in ups[-1]])
        downs.append([send(a, DOWN) for a in downs[-1]])
    xs = [own, xb, send(xa, HALF), send(xb, HALF)]
    ys = [own, yb]
    for hop in (1, 2, 3):
        ys += [ups[hop][0], downs[hop][0], ups[hop][1], downs[hop][1]]
    ys += [send(ups[3][0], UP), send(downs[3][1], DOWN)]
    carry, biases, start = None, [], 0
    for i, count in enumerate(CALLS):
        carry, bias, *message = stats(i == 0, i == 2, xs, ys[start : start + count], carry)
        biases.append(bias)
        start += count
    recv = lax.all_to_all(message[0], "blk", 0, 0)
    lses = [carry, send(carry, HALF)]
    px, py = call(pair_kernel, (valid_counts, match, own, give_y), [((N, N), F32)] * 2, smem=1)
    recv, px, py = lax.optimization_barrier((recv, px, py))
    (away,) = grads(1, recv, lses, match, xs[2:], ys, biases)
    away = send(away, HALF)
    d0, d1, row_lse, col_lse = grads(0, recv, lses, match, xs[:2], ys, biases)
    dx, dy = call(sum_kernel, (d0, d1, away), [((N, N), F32)] * 2)
    dy = send(dy, ROLE)
    grad_one, grad_two = call(
        final_kernel,
        [valid_counts, match, *lses, px, py, dx, dy],
        [((N, N), F32)] * 2,
        smem=1,
    )
    return grad_one, grad_two, row_lse.reshape(N), col_lse.reshape(N)


def solution(mesh):
    both = ("grp", "blk")
    return jax.shard_map(
        local,
        mesh=mesh,
        in_specs=(P(both, None),) * 4 + (P(both),),
        out_specs=(P(both, None), P(both, None), P(both), P(both)),
        check_vma=False,
    )
```

```python
import math

import jax
import jax.numpy as jnp
from jax import lax
from jax.experimental import pallas as pl
from jax.experimental.pallas import tpu as pltpu
from jax.sharding import PartitionSpec as P

NEG = -1e30
BF = jnp.bfloat16
F32 = jnp.float32
N = 256
SCALE2 = (2.0 / math.sqrt(256)) * math.log2(math.e)
LN2 = math.log(2.0)
NT = (((1,), (1,)), ((), ()))
NN = (((1,), (0,)), ((), ()))
MARK = 1024.0
ARRIVAL = [(0, 0), (0, 1)]
for hop in (1, 2, 3):
    ARRIVAL += [(-hop, 0), (hop, 0), (-hop, 1), (hop, 1)]
ARRIVAL += [(4, 0), (-4, 1)]
CALLS = (10, 4, 2)


def dot(a, b, dims):
    return lax.dot_general(a, b, dims, preferred_element_type=F32)


def perm(move):
    pairs = []
    for x in range(2):
        for z in range(8):
            for c in range(2):
                x2, z2, c2 = move(x, z, c)
                pairs.append(((x * 8 + z) * 2 + c, (x2 * 8 + z2 % 8) * 2 + c2))
    return pairs


ROLE = perm(lambda x, z, c: (x, z, 1 - c))
HALF = perm(lambda x, z, c: (1 - x, z, c))
UP = perm(lambda x, z, c: (x, z + 1, c))
DOWN = perm(lambda x, z, c: (x, z - 1, c))


def send(array, pairs):
    return lax.ppermute(array, "blk", pairs)


def place():
    me = lax.axis_index("blk")
    return me % 2, me // 16, (me // 2) % 8


def eye():
    return lax.broadcasted_iota(jnp.int32, (N, N), 0) == lax.broadcasted_iota(
        jnp.int32, (N, N), 1
    )


def to_column(row, diag):
    return jnp.sum(jnp.where(diag, row, 0.0), axis=1, keepdims=True)


def merge(a, b):
    top = jnp.maximum(a, b)
    return top + jnp.log2(jnp.exp2(a - top) + jnp.exp2(b - top))


def onehot(match):
    return lax.broadcasted_iota(jnp.int32, (N, N), 0) == match


def to_row(column, diag):
    return jnp.sum(jnp.where(diag, column, 0.0), axis=0, keepdims=True)


def live_column(pick, count):
    valid = lax.broadcasted_iota(jnp.int32, (N, N), 1) < count
    return jnp.sum(jnp.where(pick & valid, 1.0, 0.0), axis=1, keepdims=True) > 0.0


def x_of(ref):
    return ref[:N, :]


def y_of(ref):
    return ref[ref.shape[0] - N :, :]


def fetch(hbm, held, sems):
    copies = [
        pltpu.make_async_copy(src, dst, sems.at[i]) for i, (src, dst) in enumerate(zip(hbm, held))
    ]
    for copy in copies:
        copy.start()
    for copy in copies:
        copy.wait()


def pack_kernel(count_ref, *refs):
    hbm, outs, held, sems = refs[:4], refs[4:10], refs[10:14], refs[14]
    own_ref, x_ref, y_ref, give_x, give_y, match_ref = outs
    fetch(hbm, held, sems)
    m1, m2, f1, f2 = held

    def masked(m_ref, f_ref):
        live = live_column(onehot(m_ref[...]), count_ref[0])
        return jnp.where(live, f_ref[...].astype(F32), MARK).astype(BF)

    def write(mx, fx, my, fy):
        y = masked(my, fy)
        y_ref[...] = y
        own_ref[N:, :] = y
        own_ref[:N, :] = fx[...]
        x_ref[...] = fx[...]
        give_x[...] = masked(mx, fx)
        give_y[...] = fy[...]
        match_ref[...] = jnp.concatenate([mx[...], my[...], jnp.zeros((6, N), jnp.int32)], axis=0)

    role, _, _ = place()

    @pl.when(role == 0)
    def _():
        write(m1, f1, m2, f2)

    @pl.when(role != 0)
    def _():
        write(m2, f2, m1, f1)


def stats_kernel(first, last, *refs):
    x_refs, refs = refs[:4], refs[4:]
    if not first:
        carry_ref, refs = refs[0], refs[1:]
    outs = 3 if last else 2
    y_refs, (o_ref, bias_ref, *message_ref) = refs[:-outs], refs[-outs:]
    diag = eye()
    count = jnp.zeros((1, 1), F32) if first else carry_ref[2:3, :1]
    chunks = []
    for j in range(0, len(y_refs), 2):
        y = jnp.concatenate([y_of(y_refs[j]), y_of(y_refs[j + 1])], axis=0)
        bias = jnp.where(y[:, :1].astype(F32) > 100.0, NEG, 0.0)
        count = count + jnp.sum(jnp.where(bias < 0.0, 0.0, 1.0), axis=0, keepdims=True)
        for k in range(2):
            block = slice((j + k) * N, (j + k + 1) * N)
            bias_ref[:, block] = to_row(bias[k * N : (k + 1) * N], diag)
        chunks.append((y, bias))
    _, half, _ = place()
    for i in range(4):
        block = slice(i * N, (i + 1) * N)
        if first:
            top = jnp.full((1, N), NEG, F32)
            total = jnp.zeros((1, N), F32)
        else:
            top = carry_ref[0:1, block]
            total = carry_ref[1:2, block]
        for y, bias in chunks:
            t = dot(y, x_of(x_refs[i]), NT) * SCALE2 + bias
            new = jnp.maximum(top, jnp.max(t, axis=0, keepdims=True))
            total = total * jnp.exp2(top - new) + jnp.sum(
                jnp.exp2(t - new), axis=0, keepdims=True
            )
            top = new
        if last:
            lse = top + jnp.log2(total)
            o_ref[:, block] = lse
            rows = pl.ds((half if i < 2 else 1 - half) * 16, 16)
            message_ref[0][rows, :, (i % 2) * N : (i % 2 + 1) * N] = jnp.broadcast_to(
                lse[None], (16, 1, N)
            )
        else:
            o_ref[0:1, block] = top
            o_ref[1:2, block] = total
    if last:
        o_ref[:, 4 * N :] = jnp.broadcast_to(count, (1, 128))
    else:
        o_ref[2:3, :] = jnp.broadcast_to(count, (1, 4 * N))


def lse_row(at, own_ref, other_ref):
    other = (at + 2) % 4
    return merge(
        own_ref[:, at * N : (at + 1) * N], other_ref[:, other * N : (other + 1) * N]
    )


def lse_column(recv, z, chain):
    role, half, _ = place()
    near = slice((1 - chain) * N, (2 - chain) * N)
    source = 2 * z + 1 - role
    return merge(recv[half * 16 + source][:, near], recv[(1 - half) * 16 + source][:, near])


def bias_of(bias_refs, j):
    for ref, count in zip(bias_refs, CALLS):
        if j < count:
            return ref[:, j * N : (j + 1) * N]
        j -= count


def ordered(match, lse, diag):
    column = to_column(lse, diag)
    return jnp.sum(jnp.where(onehot(match), column, 0.0), axis=0, keepdims=True) * LN2


def grad_kernel(pair, recv, own_lse, other_lse, match_ref, x0_ref, x1_ref, *refs):
    y_refs, bias_refs, d_refs = refs[:16], refs[16:19], refs[19:]
    role, _, z = place()
    diag = eye()
    cols = [
        lse_column(recv, lax.rem(z + offset + 8, 8), chain) for offset, chain in ARRIVAL
    ]
    for i in range(2):
        row = to_column(lse_row(2 * pair + i, own_lse, other_lse), diag)
        xb = x_of((x0_ref, x1_ref)[i])
        acc = jnp.zeros((N, N), F32)
        for j, col in enumerate(cols):
            y = y_of(y_refs[j])
            t = dot(xb, y, NT) * SCALE2 + bias_of(bias_refs, j)
            w = (jnp.exp2(t - row) + jnp.exp2(t - col)).astype(BF)
            acc = acc + dot(w, y, NN)
        if pair == 0:
            d_refs[i][...] = acc
        else:
            d_refs[0][i * N : (i + 1) * N, :] = acc.astype(BF)
    if pair == 0:
        lse_x = ordered(match_ref[0:1, :], lse_row(0, own_lse, other_lse), diag)
        lse_y = ordered(match_ref[1:2, :], cols[0], diag)
        d_refs[2][...] = jnp.where(role == 0, lse_x, lse_y)
        d_refs[3][...] = jnp.where(role == 0, lse_y, lse_x)


def sum_kernel(d0_ref, d1_ref, away_ref, x_ref, y_ref):
    x_ref[...] = d0_ref[...] + away_ref[:N, :].astype(F32)
    y_ref[...] = d1_ref[...] + away_ref[N:, :].astype(F32)


def scale_of(own_lse, other_lse):
    total = own_lse[:, 4 * N :][:, :1] + other_lse[:, 4 * N :][:, :1]
    return (2.0 / math.sqrt(N)) / (2.0 * total)


def pair_kernel(count_ref, match_ref, fx_ref, fy_ref, px_ref, py_ref):
    valid = lax.broadcasted_iota(jnp.int32, (N, N), 1) < count_ref[0]
    pick_x = onehot(match_ref[0:1, :]).astype(F32)
    pick_y = onehot(match_ref[1:2, :]).astype(F32)
    to_x = dot(jnp.where(valid, pick_x, 0.0).astype(BF), pick_y.astype(BF), NT).astype(BF)
    to_y = dot(jnp.where(valid, pick_y, 0.0).astype(BF), pick_x.astype(BF), NT).astype(BF)
    px_ref[...] = dot(to_x, fy_ref[...], NN)
    py_ref[...] = dot(to_y, x_of(fx_ref), NN)


def final_kernel(count_ref, match_ref, own_lse, other_lse, px_ref, py_ref, dx_ref, dy_ref, g1, g2):
    role, _, _ = place()
    coef = scale_of(own_lse, other_lse)

    def grad_of(match, total, pair):
        live = live_column(onehot(match), count_ref[0])
        return coef * (jnp.where(live, total, 0.0) - 2.0 * pair)

    def write(gx, gy):
        gx[...] = grad_of(match_ref[0:1, :], dx_ref[...], px_ref[...])
        gy[...] = grad_of(match_ref[1:2, :], dy_ref[...], py_ref[...])

    @pl.when(role == 0)
    def _():
        write(g1, g2)

    @pl.when(role != 0)
    def _():
        write(g2, g1)


def vmem(n):
    return [pl.BlockSpec(memory_space=pltpu.VMEM)] * n


def call(kernel, ins, outs, scratch=(), smem=0, hbm=0, limit=32):
    return pl.pallas_call(
        kernel,
        out_shape=[jax.ShapeDtypeStruct(s, d) for s, d in outs],
        in_specs=[pl.BlockSpec(memory_space=pltpu.SMEM)] * smem
        + [pl.BlockSpec(memory_space=pltpu.HBM)] * hbm
        + vmem(len(ins) - smem - hbm),
        out_specs=vmem(len(outs)),
        scratch_shapes=list(scratch),
        compiler_params=pltpu.CompilerParams(vmem_limit_bytes=limit * 2**20),
        cost_estimate=pl.CostEstimate(flops=0, bytes_accessed=2**16, transcendentals=0),
    )(*ins)


def stats(first, last, xs, ys, carry):
    def kernel(*refs):
        stats_kernel(first, last, *refs)

    outs = [((1, 1152) if last else (8, 4 * N), F32), ((1, len(ys) * N), F32)]
    if last:
        outs.append(((32, 1, 2 * N), F32))
    return call(kernel, list(xs) + ([] if first else [carry]) + list(ys), outs)


def grads(pair, recv, lses, match, xs, ys, biases):
    def kernel(*refs):
        grad_kernel(pair, *refs)

    outs = [((2 * N, N), BF)] if pair else [((N, N), F32)] * 2 + [((1, N), F32)] * 2
    return call(kernel, [recv, *lses, match, *xs] + ys + biases, outs)


def local(feat_one, feat_two, match_one, match_two, valid_counts):
    held = [pltpu.VMEM((1, N), jnp.int32)] * 2 + [pltpu.VMEM((N, N), BF)] * 2
    held += [pltpu.SemaphoreType.DMA((4,))]
    own, xa, ya, give_x, give_y, match = call(
        pack_kernel,
        (valid_counts, match_one, match_two, feat_one, feat_two),
        [((2 * N, N), BF)] + [((N, N), BF)] * 4 + [((8, N), jnp.int32)],
        held,
        smem=1,
        hbm=4,
        limit=60,
    )
    yb, xb = send(give_x, ROLE), send(give_y, ROLE)
    ups, downs = [[ya, yb]], [[ya, yb]]
    for hop in range(3):
        ups.append([send(a, UP) for a in ups[-1]])
        downs.append([send(a, DOWN) for a in downs[-1]])
    xd, downs[1][0] = lax.optimization_barrier((xb, downs[1][0]))
    xs = [own, xb, send(xa, HALF), send(xd, HALF)]
    ys = [own, yb]
    for hop in (1, 2, 3):
        ys += [ups[hop][0], downs[hop][0], ups[hop][1], downs[hop][1]]
    ys += [send(downs[3][0], DOWN), send(ups[3][1], UP)]
    carry, biases, start = None, [], 0
    for i, count in enumerate(CALLS):
        carry, bias, *message = stats(i == 0, i == 2, xs, ys[start : start + count], carry)
        biases.append(bias)
        start += count
    recv = lax.all_to_all(message[0], "blk", 0, 0)
    lses = [carry, send(carry, HALF)]
    px, py = call(pair_kernel, (valid_counts, match, own, give_y), [((N, N), F32)] * 2, smem=1)
    recv, px, py = lax.optimization_barrier((recv, px, py))
    (away,) = grads(1, recv, lses, match, xs[2:], ys, biases)
    away = send(away, HALF)
    d0, d1, row_lse, col_lse = grads(0, recv, lses, match, xs[:2], ys, biases)
    dx, dy = call(sum_kernel, (d0, d1, away), [((N, N), F32)] * 2)
    dy = send(dy, ROLE)
    grad_one, grad_two = call(
        final_kernel,
        [valid_counts, match, *lses, px, py, dx, dy],
        [((N, N), F32)] * 2,
        smem=1,
    )
    return grad_one, grad_two, row_lse.reshape(N), col_lse.reshape(N)


def solution(mesh):
    both = ("grp", "blk")
    return jax.shard_map(
        local,
        mesh=mesh,
        in_specs=(P(both, None),) * 4 + (P(both),),
        out_specs=(P(both, None), P(both, None), P(both), P(both)),
        check_vma=False,
    )
```

```python
import math

import jax
import jax.numpy as jnp
from jax import lax
from jax.experimental import pallas as pl
from jax.experimental.pallas import tpu as pltpu
from jax.sharding import PartitionSpec as P

NEG = -1e30
BF = jnp.bfloat16
F32 = jnp.float32
N = 256
SCALE2 = (2.0 / math.sqrt(256)) * math.log2(math.e)
LN2 = math.log(2.0)
NT = (((1,), (1,)), ((), ()))
NN = (((1,), (0,)), ((), ()))
MARK = 1024.0
ARRIVAL = [(0, 0), (0, 1)]
for hop in (1, 2, 3):
    ARRIVAL += [(-hop, 0), (hop, 0), (-hop, 1), (hop, 1)]
ARRIVAL += [(4, 0), (-4, 1)]
CALLS = (10, 4, 2)


def dot(a, b, dims):
    return lax.dot_general(a, b, dims, preferred_element_type=F32)


def perm(move):
    pairs = []
    for x in range(2):
        for z in range(8):
            for c in range(2):
                x2, z2, c2 = move(x, z, c)
                pairs.append(((x * 8 + z) * 2 + c, (x2 * 8 + z2 % 8) * 2 + c2))
    return pairs


ROLE = perm(lambda x, z, c: (x, z, 1 - c))
HALF = perm(lambda x, z, c: (1 - x, z, c))
UP = perm(lambda x, z, c: (x, z + 1, c))
DOWN = perm(lambda x, z, c: (x, z - 1, c))


def send(array, pairs):
    return lax.ppermute(array, "blk", pairs)


def place():
    me = lax.axis_index("blk")
    return me % 2, me // 16, (me // 2) % 8


def eye():
    return lax.broadcasted_iota(jnp.int32, (N, N), 0) == lax.broadcasted_iota(
        jnp.int32, (N, N), 1
    )


def to_column(row, diag):
    return jnp.sum(jnp.where(diag, row, 0.0), axis=1, keepdims=True)


def merge(a, b):
    top = jnp.maximum(a, b)
    return top + jnp.log2(jnp.exp2(a - top) + jnp.exp2(b - top))


def onehot(match):
    return lax.broadcasted_iota(jnp.int32, (N, N), 0) == match


def to_row(column, diag):
    return jnp.sum(jnp.where(diag, column, 0.0), axis=0, keepdims=True)


def live_column(pick, count):
    valid = lax.broadcasted_iota(jnp.int32, (N, N), 1) < count
    return jnp.sum(jnp.where(pick & valid, 1.0, 0.0), axis=1, keepdims=True) > 0.0


def x_of(ref):
    return ref[:N, :]


def y_of(ref):
    return ref[ref.shape[0] - N :, :]


def pack_kernel(count_ref, *refs):
    hbm, outs, held, sems = refs[:4], refs[4:10], refs[10:14], refs[14]
    own_ref, x_ref, y_ref, give_x, give_y, match_ref = outs
    copies = [
        pltpu.make_async_copy(src, dst, sems.at[i]) for i, (src, dst) in enumerate(zip(hbm, held))
    ]
    for copy in copies:
        copy.start()
    m1, m2, f1, f2 = held
    copies[0].wait()
    copies[1].wait()
    live1 = live_column(onehot(m1[...]), count_ref[0])
    live2 = live_column(onehot(m2[...]), count_ref[0])
    copies[2].wait()
    copies[3].wait()

    def masked(live, f_ref):
        return jnp.where(live, f_ref[...].astype(F32), MARK).astype(BF)

    def write(mx, lx, fx, my, ly, fy):
        y = masked(ly, fy)
        y_ref[...] = y
        own_ref[N:, :] = y
        own_ref[:N, :] = fx[...]
        x_ref[...] = fx[...]
        give_x[...] = masked(lx, fx)
        give_y[...] = fy[...]
        match_ref[...] = jnp.concatenate([mx[...], my[...], jnp.zeros((6, N), jnp.int32)], axis=0)

    role, _, _ = place()

    @pl.when(role == 0)
    def _():
        write(m1, live1, f1, m2, live2, f2)

    @pl.when(role != 0)
    def _():
        write(m2, live2, f2, m1, live1, f1)


def stats_kernel(first, last, *refs):
    x_refs, refs = refs[:4], refs[4:]
    if not first:
        carry_ref, refs = refs[0], refs[1:]
    outs = 3 if last else 2
    y_refs, (o_ref, bias_ref, *message_ref) = refs[:-outs], refs[-outs:]
    diag = eye()
    count = jnp.zeros((1, 1), F32) if first else carry_ref[2:3, :1]
    chunks = []
    for j in range(0, len(y_refs), 2):
        y = jnp.concatenate([y_of(y_refs[j]), y_of(y_refs[j + 1])], axis=0)
        bias = jnp.where(y[:, :1].astype(F32) > 100.0, NEG, 0.0)
        count = count + jnp.sum(jnp.where(bias < 0.0, 0.0, 1.0), axis=0, keepdims=True)
        for k in range(2):
            block = slice((j + k) * N, (j + k + 1) * N)
            bias_ref[:, block] = to_row(bias[k * N : (k + 1) * N], diag)
        chunks.append((y, bias))
    _, half, _ = place()
    for i in range(4):
        block = slice(i * N, (i + 1) * N)
        if first:
            top = jnp.full((1, N), NEG, F32)
            total = jnp.zeros((1, N), F32)
        else:
            top = carry_ref[0:1, block]
            total = carry_ref[1:2, block]
        for y, bias in chunks:
            t = dot(y, x_of(x_refs[i]), NT) * SCALE2 + bias
            new = jnp.maximum(top, jnp.max(t, axis=0, keepdims=True))
            total = total * jnp.exp2(top - new) + jnp.sum(
                jnp.exp2(t - new), axis=0, keepdims=True
            )
            top = new
        if last:
            lse = top + jnp.log2(total)
            o_ref[:, block] = lse
            rows = pl.ds((half if i < 2 else 1 - half) * 16, 16)
            message_ref[0][rows, :, (i % 2) * N : (i % 2 + 1) * N] = jnp.broadcast_to(
                lse[None], (16, 1, N)
            )
        else:
            o_ref[0:1, block] = top
            o_ref[1:2, block] = total
    if last:
        o_ref[:, 4 * N :] = jnp.broadcast_to(count, (1, 128))
    else:
        o_ref[2:3, :] = jnp.broadcast_to(count, (1, 4 * N))


def lse_row(at, own_ref, other_ref):
    other = (at + 2) % 4
    return merge(
        own_ref[:, at * N : (at + 1) * N], other_ref[:, other * N : (other + 1) * N]
    )


def lse_column(recv, z, chain):
    role, half, _ = place()
    near = slice((1 - chain) * N, (2 - chain) * N)
    source = 2 * z + 1 - role
    return merge(recv[half * 16 + source][:, near], recv[(1 - half) * 16 + source][:, near])


def bias_of(bias_refs, j):
    for ref, count in zip(bias_refs, CALLS):
        if j < count:
            return ref[:, j * N : (j + 1) * N]
        j -= count


def ordered(match, lse, diag):
    column = to_column(lse, diag)
    return jnp.sum(jnp.where(onehot(match), column, 0.0), axis=0, keepdims=True) * LN2


def grad_kernel(pair, recv, own_lse, other_lse, match_ref, x0_ref, x1_ref, *refs):
    y_refs, bias_refs, d_refs = refs[:16], refs[16:19], refs[19:]
    role, _, z = place()
    diag = eye()
    cols = [
        lse_column(recv, lax.rem(z + offset + 8, 8), chain) for offset, chain in ARRIVAL
    ]
    for i in range(2):
        row = to_column(lse_row(2 * pair + i, own_lse, other_lse), diag)
        xb = x_of((x0_ref, x1_ref)[i])
        acc = jnp.zeros((N, N), F32)
        for j, col in enumerate(cols):
            y = y_of(y_refs[j])
            t = dot(xb, y, NT) * SCALE2 + bias_of(bias_refs, j)
            w = (jnp.exp2(t - row) + jnp.exp2(t - col)).astype(BF)
            acc = acc + dot(w, y, NN)
        if pair == 0:
            d_refs[i][...] = acc
        else:
            d_refs[0][i * N : (i + 1) * N, :] = acc.astype(BF)
    if pair == 0:
        lse_x = ordered(match_ref[0:1, :], lse_row(0, own_lse, other_lse), diag)
        lse_y = ordered(match_ref[1:2, :], cols[0], diag)
        d_refs[2][...] = jnp.where(role == 0, lse_x, lse_y)
        d_refs[3][...] = jnp.where(role == 0, lse_y, lse_x)


def sum_kernel(d0_ref, d1_ref, away_ref, x_ref, y_ref):
    x_ref[...] = d0_ref[...] + away_ref[:N, :].astype(F32)
    y_ref[...] = d1_ref[...] + away_ref[N:, :].astype(F32)


def scale_of(own_lse, other_lse):
    total = own_lse[:, 4 * N :][:, :1] + other_lse[:, 4 * N :][:, :1]
    return (2.0 / math.sqrt(N)) / (2.0 * total)


def pair_kernel(count_ref, match_ref, fx_ref, fy_ref, px_ref, py_ref):
    valid = lax.broadcasted_iota(jnp.int32, (N, N), 1) < count_ref[0]
    pick_x = onehot(match_ref[0:1, :]).astype(F32)
    pick_y = onehot(match_ref[1:2, :]).astype(F32)
    to_x = dot(jnp.where(valid, pick_x, 0.0).astype(BF), pick_y.astype(BF), NT).astype(BF)
    to_y = dot(jnp.where(valid, pick_y, 0.0).astype(BF), pick_x.astype(BF), NT).astype(BF)
    px_ref[...] = dot(to_x, fy_ref[...], NN)
    py_ref[...] = dot(to_y, x_of(fx_ref), NN)


def final_kernel(count_ref, match_ref, own_lse, other_lse, px_ref, py_ref, dx_ref, dy_ref, g1, g2):
    role, _, _ = place()
    coef = scale_of(own_lse, other_lse)

    def grad_of(match, total, pair):
        live = live_column(onehot(match), count_ref[0])
        return coef * (jnp.where(live, total, 0.0) - 2.0 * pair)

    def write(gx, gy):
        gx[...] = grad_of(match_ref[0:1, :], dx_ref[...], px_ref[...])
        gy[...] = grad_of(match_ref[1:2, :], dy_ref[...], py_ref[...])

    @pl.when(role == 0)
    def _():
        write(g1, g2)

    @pl.when(role != 0)
    def _():
        write(g2, g1)


def vmem(n):
    return [pl.BlockSpec(memory_space=pltpu.VMEM)] * n


def call(kernel, ins, outs, scratch=(), smem=0, hbm=0, limit=32):
    return pl.pallas_call(
        kernel,
        out_shape=[jax.ShapeDtypeStruct(s, d) for s, d in outs],
        in_specs=[pl.BlockSpec(memory_space=pltpu.SMEM)] * smem
        + [pl.BlockSpec(memory_space=pltpu.HBM)] * hbm
        + vmem(len(ins) - smem - hbm),
        out_specs=vmem(len(outs)),
        scratch_shapes=list(scratch),
        compiler_params=pltpu.CompilerParams(vmem_limit_bytes=limit * 2**20),
        cost_estimate=pl.CostEstimate(flops=0, bytes_accessed=2**16, transcendentals=0),
    )(*ins)


def stats(first, last, xs, ys, carry):
    def kernel(*refs):
        stats_kernel(first, last, *refs)

    outs = [((1, 1152) if last else (8, 4 * N), F32), ((1, len(ys) * N), F32)]
    if last:
        outs.append(((32, 1, 2 * N), F32))
    return call(kernel, list(xs) + ([] if first else [carry]) + list(ys), outs)


def grads(pair, recv, lses, match, xs, ys, biases):
    def kernel(*refs):
        grad_kernel(pair, *refs)

    outs = [((2 * N, N), BF)] if pair else [((N, N), F32)] * 2 + [((1, N), F32)] * 2
    return call(kernel, [recv, *lses, match, *xs] + ys + biases, outs)


def local(feat_one, feat_two, match_one, match_two, valid_counts):
    held = [pltpu.VMEM((1, N), jnp.int32)] * 2 + [pltpu.VMEM((N, N), BF)] * 2
    held += [pltpu.SemaphoreType.DMA((4,))]
    own, xa, ya, give_x, give_y, match = call(
        pack_kernel,
        (valid_counts, match_one, match_two, feat_one, feat_two),
        [((2 * N, N), BF)] + [((N, N), BF)] * 4 + [((8, N), jnp.int32)],
        held,
        smem=1,
        hbm=4,
        limit=60,
    )
    yb, xb = send(give_x, ROLE), send(give_y, ROLE)
    ups, downs = [[ya, yb]], [[ya, yb]]
    for hop in range(3):
        ups.append([send(a, UP) for a in ups[-1]])
        downs.append([send(a, DOWN) for a in downs[-1]])
    xd, downs[1][0] = lax.optimization_barrier((xb, downs[1][0]))
    xs = [own, xb, send(xa, HALF), send(xd, HALF)]
    ys = [own, yb]
    for hop in (1, 2, 3):
        ys += [ups[hop][0], downs[hop][0], ups[hop][1], downs[hop][1]]
    ys += [send(downs[3][0], DOWN), send(ups[3][1], UP)]
    carry, biases, start = None, [], 0
    for i, count in enumerate(CALLS):
        carry, bias, *message = stats(i == 0, i == 2, xs, ys[start : start + count], carry)
        biases.append(bias)
        start += count
    recv = lax.all_to_all(message[0], "blk", 0, 0)
    lses = [carry, send(carry, HALF)]
    px, py = call(pair_kernel, (valid_counts, match, own, give_y), [((N, N), F32)] * 2, smem=1)
    recv, px, py = lax.optimization_barrier((recv, px, py))
    (away,) = grads(1, recv, lses, match, xs[2:], ys, biases)
    away = send(away, HALF)
    d0, d1, row_lse, col_lse = grads(0, recv, lses, match, xs[:2], ys, biases)
    dx, dy = call(sum_kernel, (d0, d1, away), [((N, N), F32)] * 2)
    dy = send(dy, ROLE)
    grad_one, grad_two = call(
        final_kernel,
        [valid_counts, match, *lses, px, py, dx, dy],
        [((N, N), F32)] * 2,
        smem=1,
    )
    return grad_one, grad_two, row_lse.reshape(N), col_lse.reshape(N)


def solution(mesh):
    both = ("grp", "blk")
    return jax.shard_map(
        local,
        mesh=mesh,
        in_specs=(P(both, None),) * 4 + (P(both),),
        out_specs=(P(both, None), P(both, None), P(both), P(both)),
        check_vma=False,
    )
```
